32 devices in a mesh: grp: 2 (over y), lon: 16 (over z, x, core).
Axes of the slice: x: 2, y: 2, z: 4, core: 2. Of those that a mesh axis runs over, the one named last changes fastest.
Arguments:
- ocean_state: float32 [4, 16, 128, 128], P(None, 'grp', 'lon'), parts along dimension 1, may hold values from -4 to 4
- ocean_mask: int32 [128, 128], P('lon'), may hold values 0 or 1
- polar_rows: int32 [8], replicated, may hold values from 112 to 127, as said below
- target_state: float32 [4, 16, 128, 128], P(None, 'grp', 'lon'), parts along dimension 1, may hold values from -6 to 6
- weight_in: float32 [64, 3], replicated, may hold values from -3.5 to 3.5
- bias_in: float32 [64], replicated, may hold values from -0.5 to 0.5
- weight_mid: float32 [64, 64], replicated, may hold values from -0.75 to 0.75
- bias_mid: float32 [64], replicated, may hold values from -0.5 to 0.5
- weight_out: float32 [3, 64], replicated, may hold values from -0.75 to 0.75
Outputs:
- final_state: float32 [4, 16, 128, 128], P(None, 'grp', 'lon'), parts along dimension 1
- middle_sensitivity: float32 [4, 16, 128, 128], P(None, 'grp', 'lon'), parts along dimension 1
- grad_weight_in: float32 [128, 3], P('grp'), parts along dimension 0
- grad_bias_in: float32 [128], P('grp'), parts along dimension 0
- grad_weight_mid: float32 [128, 64], P('grp'), parts along dimension 0
- grad_bias_mid: float32 [128], P('grp'), parts along dimension 0
- grad_weight_out: float32 [6, 64], P('grp'), parts along dimension 0
The draws below stay inside these ranges and needn't reach their ends.
There are 2 independent parts, one for each index of `grp`. The reference program is written for one: setup_inputs(seed, part) draws one part's arguments, and reference() takes and returns one part's arrays. A program takes and returns all parts, laid end to end along the dimension named above; an argument that names none is the same for every part. Nothing has to cross between parts.
Inputs may be any that keep to these rules, and one draw needn't show every extreme that they name: `polar_rows`: 8 distinct rows in increasing order, the j-th being 128 - 2 * 8 + 2 j or the row after it.
All inputs are finite; a program needn't handle non-finite values. No bound on the sum of `ocean_mask` on one device may be relied on, other than what follows from the above.
Results may differ from the reference program's by a relative error of at most 0.000098.
Values sent between devices are 32-bit elements; how exact they have to be, the bound alone decides.
A program may use at most 128 MiB of HBM per device.

```python
import jax
import jax.numpy as jnp
from jax import lax

LON_DEV = 8
LAT = 128
KZ = 8
HID = 64
NPOLE = 8
NLON = 128


def draw_polar_rows(key, part):
    choose_bits = jax.random.randint(key, (NPOLE,), 0, 2)
    choose_bits = choose_bits.at[0].set(0).at[NPOLE - 1].set(1)
    return (LAT - 2 * NPOLE + 2 * jnp.arange(NPOLE) + choose_bits).astype(jnp.int32)


def draw_ocean_state(key, part):
    noise = jax.random.normal(key, (4, KZ, NLON, LAT), jnp.float32)
    return jnp.clip(noise, -4.0, 4.0)


def touch_ends(array, own_key, low, top_value):
    longest = array.shape.index(max(array.shape))
    spots = []
    for shift in (0, 1):
        where = [jax.random.randint(jax.random.fold_in(own_key, axis), (), 0, length) for axis, length in enumerate(array.shape)]
        where[longest] = (where[longest] + shift) % array.shape[longest]
        spots.append(tuple(where))
    return array.at[spots[0]].set(low).at[spots[1]].set(top_value)


def block_levels(key, dims, pieces, least, high):
    def one(axis_at, shards_of):
        heights = jax.random.uniform(jax.random.fold_in(jax.random.fold_in(key, 6), axis_at), (shards_of,), jnp.float32, least / len(pieces), high / len(pieces))
        return jnp.repeat(jnp.exp(heights), dims[axis_at] // shards_of).reshape((-1,) + (1,) * (len(dims) - axis_at - 1))

    level = one(*pieces[0])
    for cut in pieces[1:]:
        level = level * one(*cut)
    return level


def normal_values(key, dims, width, most, split=(), held_as=jnp.bfloat16):
    array = jax.random.normal(key, dims, jnp.float32) * width
    if len(split) > 0:
        array = block_levels(key, dims, split, -0.22, 0.18) * array
    return jnp.clip(array, min=-most, max=most).astype(held_as)


def setup_inputs(seed: int = 0, part: int = 0) -> dict:
    key_of = jax.random.split(jax.random.key(seed), 10)
    part_keys = jax.random.split(jax.random.fold_in(key_of[9], part), 10)
    ocean_state = draw_ocean_state(jax.random.fold_in(jax.random.fold_in(key_of[9], part), 71), part)
    ocean_mask = touch_ends((jax.random.randint(key_of[1], (NLON, LAT), 0, 8) < 7).astype(jnp.int32), jax.random.fold_in(key_of[1], 1), 0, 1)
    polar_rows = draw_polar_rows(jax.random.fold_in(key_of[9], 71), part)
    target_state = normal_values(part_keys[3], (4, KZ, NLON, LAT), 1.0, 6.0, ((2, 16),), jnp.float32)
    weight_in = normal_values(key_of[4], (HID, 3), 3 ** -0.5, 3.5, (), jnp.float32)
    bias_in = jnp.clip(jax.random.uniform(key_of[5], (HID,), jnp.float32, -0.5, 0.5), -0.5, 0.5)
    weight_mid = normal_values(key_of[6], (HID, HID), HID ** -0.5, 0.75, (), jnp.float32)
    bias_mid = jnp.clip(jax.random.uniform(key_of[7], (HID,), jnp.float32, -0.5, 0.5), -0.5, 0.5)
    weight_out = normal_values(key_of[8], (3, HID), HID ** -0.5, 0.75, (), jnp.float32)
    return dict(ocean_state=ocean_state, ocean_mask=ocean_mask, polar_rows=polar_rows, target_state=target_state, weight_in=weight_in, bias_in=bias_in, weight_mid=weight_mid, bias_mid=bias_mid, weight_out=weight_out)


TIME_INCREMENT = 0.2
VISCOSITY = 0.05
SCALAR_SPREADING = 0.05
PRESSURE_GAIN = 0.3
CLOSURE_GAIN = 0.3

def eastward_axis(grid_field):
    return 0.5 * (grid_field[:, 2:] - grid_field[:, :-2])

def northward_axis(grid_field):
    padded = jnp.pad(grid_field, ((0, 0), (0, 0), (1, 1)))
    return 0.5 * (padded[:, :, 2:] - padded[:, :, :-2])

def second_derivative_sum(grid_field):
    padded = jnp.pad(grid_field, ((0, 0), (0, 0), (1, 1)))
    return grid_field[:, 2:] + grid_field[:, :-2] + padded[:, 1:-1, 2:] + padded[:, 1:-1, :-2] - 4.0 * grid_field[:, 1:-1]

def closure_level(features, weights):
    weight_in, bias_in, weight_mid, bias_mid, weight_out = weights
    highest = lax.Precision.HIGHEST
    first_layer = jnp.tanh(jnp.dot(weight_in, features, precision=highest, preferred_element_type=jnp.float32) + bias_in[:, None])
    second_layer = jnp.tanh(jnp.dot(weight_mid, first_layer, precision=highest, preferred_element_type=jnp.float32) + bias_mid[:, None])
    return CLOSURE_GAIN * jnp.dot(weight_out, second_layer, precision=highest, preferred_element_type=jnp.float32)

def tendency(haloed_lattice, water_point_indicator, coriolis, weights):
    eastward_flow, northward_flow, heat_content_values, saltiness_values = (haloed_lattice[0], haloed_lattice[1], haloed_lattice[2], haloed_lattice[3])
    zonal_inner = eastward_flow[:, 1:-1]
    merid_inner = northward_flow[:, 1:-1]
    zonal_dx = eastward_axis(eastward_flow)
    merid_dx = eastward_axis(northward_flow)
    zonal_dy = northward_axis(zonal_inner)
    merid_dy = northward_axis(merid_inner)
    vorticity = merid_dx - zonal_dy
    shearing = zonal_dy + merid_dx
    stretching = zonal_dx - merid_dy
    features = jnp.stack([vorticity, shearing, stretching], 1)
    levels, _, columns_ext, lat_rows = features.shape
    flattened = features.reshape(levels, 3, columns_ext * lat_rows)
    per_level = jax.checkpoint(closure_level)
    stress = lax.map(lambda level_features: per_level(level_features, weights), flattened)
    stress = stress.reshape(levels, 3, columns_ext, lat_rows)
    force_x = eastward_axis(stress[:, 0]) + northward_axis(stress[:, 1, 1:-1])
    force_y = eastward_axis(stress[:, 1]) + northward_axis(stress[:, 2, 1:-1])
    density_anomaly_map = 0.6 * heat_content_values - 0.4 * saltiness_values
    eastward_flow_core = eastward_flow[:, 2:-2]
    northward_flow_core = northward_flow[:, 2:-2]
    heat_content_core = heat_content_values[:, 2:-2]
    salt_core = saltiness_values[:, 2:-2]
    eastward_flow_updated = water_point_indicator * (eastward_flow_core + TIME_INCREMENT * (coriolis * northward_flow_core - PRESSURE_GAIN * eastward_axis(density_anomaly_map[:, 1:-1]) + force_x + VISCOSITY * second_derivative_sum(zonal_inner)))
    northward_flow_updated = water_point_indicator * (northward_flow_core + TIME_INCREMENT * (-coriolis * eastward_flow_updated - PRESSURE_GAIN * northward_axis(density_anomaly_map[:, 2:-2]) + force_y + VISCOSITY * second_derivative_sum(merid_inner)))
    heat_content_updated = water_point_indicator * (heat_content_core + TIME_INCREMENT * (-eastward_flow_core * eastward_axis(heat_content_values[:, 1:-1]) - northward_flow_core * northward_axis(heat_content_core) + SCALAR_SPREADING * second_derivative_sum(heat_content_values[:, 1:-1])))
    saltiness_updated = water_point_indicator * (salt_core + TIME_INCREMENT * (-eastward_flow_core * eastward_axis(saltiness_values[:, 1:-1]) - northward_flow_core * northward_axis(salt_core) + SCALAR_SPREADING * second_derivative_sum(saltiness_values[:, 1:-1])))
    return jnp.stack([eastward_flow_updated, northward_flow_updated, heat_content_updated, saltiness_updated])

def polar_filter(grid_field, polar_rows, strength):
    picked = jnp.take(grid_field, polar_rows, axis=3)
    loop_length = picked.shape[2]
    wavenumber = jnp.arange(loop_length // 2 + 1).astype(jnp.float32)
    eigenvalue = 1.0 + 2.0 * strength[None, :] * (1.0 - jnp.cos(2.0 * jnp.pi * wavenumber[:, None] / loop_length))
    spectrum = jnp.fft.rfft(picked, axis=2) / eigenvalue
    filtered_rows = jnp.fft.irfft(spectrum, n=loop_length, axis=2).astype(grid_field.dtype)
    return grid_field.at[:, :, :, polar_rows].set(filtered_rows)

def reference(ocean_state, ocean_mask, polar_rows, target_state, weight_in, bias_in, weight_mid, bias_mid, weight_out):
    water_point_indicator = ocean_mask.astype(jnp.float32)
    coriolis = 0.5 + 0.5 * (jnp.arange(LAT).astype(jnp.float32) + 0.5) / LAT
    first_row = LAT - 2 * NPOLE
    lon_count = ocean_state.shape[2]
    strength = (lon_count / 8.0) ** 2 * (2.0 + 4.0 * (polar_rows - first_row).astype(jnp.float32) / (2 * NPOLE))
    lon_weight = 1.0 + 2.0 * jnp.arange(lon_count).astype(jnp.float32) / lon_count
    scaling = 1.0 / (KZ * LAT * LON_DEV)
    unscaling = float(KZ * LAT * LON_DEV)

    def one_step(current, weights):
        haloed_lattice = jnp.concatenate([current[:, :, -2:], current, current[:, :, :2]], 2)
        return polar_filter(tendency(haloed_lattice, water_point_indicator, coriolis, weights), polar_rows, strength)

    def tail_run(weights, middle_state):
        final_state = one_step(middle_state, weights)
        mismatch = final_state - target_state
        misfit = 0.5 * scaling * jnp.sum(lon_weight[:, None] * mismatch * mismatch)
        return (misfit, final_state)
    weights = (weight_in, bias_in, weight_mid, bias_mid, weight_out)
    middle_state, pull_first = jax.vjp(lambda params: one_step(ocean_state, params), weights)
    misfit, pull_second, final_state = jax.vjp(tail_run, weights, middle_state, has_aux=True)
    grads_second, middle_grad = pull_second(jnp.ones_like(misfit))
    grads_first = pull_first(middle_grad)[0]
    grads = tuple((late + early for late, early in zip(grads_second, grads_first)))
    return (final_state, middle_grad * unscaling, grads[0], grads[1], grads[2], grads[3], grads[4])
```

```python
import functools

import jax
import jax.numpy as jnp
import numpy as np
from jax import lax
from jax.experimental import pallas as pl
from jax.experimental.pallas import tpu as pltpu
from jax.sharding import PartitionSpec as P

DT = 0.2
VISC = 0.05
PRESS = 0.3
GAIN = 0.3
F32 = jnp.float32
BF16 = jnp.bfloat16
MESH = pl.DeviceIdType.MESH


def filter_tables(n, width, lat, pole):
    total = n * width
    band = 2 * pole
    rows = np.arange(band, dtype=np.float64)
    k = (total / 8.0) ** 2 * (2.0 + 4.0 * rows / band)
    theta = 2.0 * np.arcsinh(0.5 / np.sqrt(k))
    power = lambda d: np.exp(-theta * d)
    norm = (1.0 - power(total)) * np.sqrt(1.0 + 4.0 * k)
    wide = lambda x: np.concatenate([np.zeros(lat - band), x])
    i = range(width)
    local = [wide((power(d) + power(total - d)) / norm) for d in i]
    east = [wide(power(width - 1 - d)) for d in i]
    west = [wide(power(d)) for d in i]
    from_west = [wide(power(d + 1) / norm) for d in i]
    from_east = [wide(power(width - d) / norm) for d in i]
    inverse = [wide(1.0 / k)]
    table = np.stack(local + east + west + from_west + from_east + inverse)
    table = np.broadcast_to(table[:, None, :], (len(table), 8, lat))
    hops = np.stack(
        [
            np.concatenate([power(width * (m - 1))] * 4 + [power(width * (n - m - 1))] * 4)
            for m in range(1, n)
        ]
    )
    hops = np.broadcast_to(hops[:, None, :], (n - 1, 8, lat))
    return table.astype(np.float32), hops.astype(np.float32)


def split(a):
    high = a.astype(BF16)
    return high, (a - high.astype(F32)).astype(BF16)


def dot3(a, b, transposed=False):
    dims = (((1,), (1 if transposed else 0,)), ((), ()))
    mul = lambda x, y: lax.dot_general(x, y, dims, preferred_element_type=F32)
    return mul(a[0], b[0]) + (mul(a[0], b[1]) + mul(a[1], b[0]))


def kernel(
    n,
    rows_ref,
    state_ref,
    mask_ref,
    target_ref,
    win_ref,
    wint_ref,
    bin_ref,
    wmid_ref,
    wmidt_ref,
    bmid_ref,
    wout_ref,
    woutt_ref,
    tab_ref,
    hop_ref,
    final_ref,
    sens_ref,
    grad_ref,
    ext1,
    raw,
    ext2,
    adj,
    rim,
    upd,
    feat,
    stress,
    hid1,
    hid2,
    sendv,
    recvv,
    gsend,
    grecv,
    halo_send,
    halo_recv,
    fil_send,
    fil_recv,
    red_send,
    red_recv,
):
    width = 8
    lat = 128
    me = lax.axis_index("lon")
    left, right = lax.rem(me + n - 1, n), lax.rem(me + 1, n)
    lane = lax.broadcasted_iota(jnp.int32, (1, 1, lat), 2)
    lane2 = lax.broadcasted_iota(jnp.int32, (8, lat), 1)
    steps = n.bit_length() - 1

    barrier = pltpu.get_barrier_semaphore()

    def greet(m, carry):
        pl.semaphore_signal(
            barrier, inc=1, device_id={"lon": lax.rem(me + m, n)}, device_id_type=MESH
        )
        return carry

    lax.fori_loop(1, n, greet, 0)

    for f in range(4):
        for i in range(width):
            ext1[2 + i, f] = state_ref[f, :, i, :]
    pl.semaphore_wait(barrier, n - 1)

    def remote(src, dst, ssem, rsem, dev):
        return pltpu.make_async_remote_copy(
            src_ref=src, dst_ref=dst, send_sem=ssem, recv_sem=rsem,
            device_id={"lon": dev}, device_id_type=MESH,
        )

    def exchange(which, src_l, src_r, dst_l, dst_r):
        a = remote(src_l, dst_l, halo_send.at[which, 0], halo_recv.at[which, 0], left)
        b = remote(src_r, dst_r, halo_send.at[which, 1], halo_recv.at[which, 1], right)
        a.start()
        b.start()
        return a, b

    def halo(which, ref):
        return exchange(
            which,
            ref.at[pl.ds(2, 2)],
            ref.at[pl.ds(8, 2)],
            ref.at[pl.ds(10, 2)],
            ref.at[pl.ds(0, 2)],
        )

    def finish(pair):
        for c in pair:
            c.wait()

    first_halo = halo(0, ext1)

    polar = lane2 == rows_ref[0]
    for j in range(1, rows_ref.shape[0]):
        polar = jnp.logical_or(polar, lane2 == rows_ref[j])
    wet = jnp.broadcast_to(mask_ref[...].astype(F32), (width, 8, lat))
    cor = 0.5 + 0.5 * (lane.astype(F32) + 0.5) / lat
    local = [
        jnp.where(polar, tab_ref[d], 1.0 if d == 0 else 0.0) for d in range(width)
    ]
    inv_k = tab_ref[5 * width]

    def dy_sides(x):
        up = jnp.where(lane == lat - 1, 0.0, pltpu.roll(x, lat - 1, 2))
        down = jnp.where(lane == 0, 0.0, pltpu.roll(x, 1, 2))
        return up, down

    def dy(x):
        up, down = dy_sides(x)
        return 0.5 * (up - down)

    def dx(x):
        return 0.5 * (x[2:] - x[:-2])

    def lap(x):
        up, down = dy_sides(x[1:-1])
        return x[2:] + x[:-2] + up + down - 4.0 * x[1:-1]

    def pad(x, count=1):
        zero = jnp.zeros((count,) + x.shape[1:], F32)
        return jnp.concatenate([zero, x, zero], 0)

    def dx_t(x):
        wide = pad(x, 2)
        return -0.5 * (wide[2:] - wide[:-2])

    def lap_t(x):
        return lap(pad(x, 2))

    def filter_start(which, b):
        packed = jnp.zeros((8, lat), F32)
        for q in range(8):
            f = q % 4
            base = width if q < 4 else 2 * width
            moment = b[0][f] * tab_ref[base]
            for i in range(1, width):
                moment += b[i][f] * tab_ref[base + i]
            shift = (16 * q + 16) % lat
            packed += pltpu.roll(moment, shift, 1) if shift else moment
        sendv[which] = packed

        def push(m, carry):
            remote(
                sendv.at[which], recvv.at[which, m - 1],
                fil_send.at[which], fil_recv.at[which], lax.rem(me + m, n),
            ).start()
            return carry

        lax.fori_loop(1, n, push, 0)

    def filter_finish(which, b):
        out = []
        for i in range(width):
            cols = []
            for f in range(4):
                acc = local[i] * b[0][f]
                for j in range(1, width):
                    acc += local[abs(i - j)] * b[j][f]
                cols.append(acc)
            out.append(cols)
        whole = remote(
            recvv.at[which], recvv.at[which], fil_send.at[which], fil_recv.at[which], right
        )
        whole.wait_recv()
        whole.wait_send()
        total = jnp.sum(recvv[which] * hop_ref[...], axis=0)
        for f in range(4):
            parts = []
            for q in (f, f + 4):
                shift = (lat - 16 - 16 * q) % lat
                parts.append(pltpu.roll(total, shift, 1) if shift else total)
            for i in range(width):
                out[i][f] = out[i][f] + jnp.where(
                    polar,
                    tab_ref[3 * width + i] * parts[0] + tab_ref[4 * width + i] * parts[1],
                    0.0,
                )
        return out

    columns = width + 2
    win = win_ref[...]
    woutt = woutt_ref[...]
    bias_in = bin_ref[...]
    bias_mid = bmid_ref[...]

    def closure(step, ext):
        u, v = ext[:, 0], ext[:, 1]
        du, dv = dx(u), dx(v)
        eu, ev = dy(u[1:-1]), dy(v[1:-1])
        x = (dv - eu, eu + dv, du - ev)
        for c in range(3):
            for e in range(columns):
                feat[step, :, c, e * lat : (e + 1) * lat] = x[c][e]
        feat[step, :, 3, :] = jnp.ones((8, columns * lat), F32)
        feat[step, :, 4:8, :] = jnp.zeros((8, 4, columns * lat), F32)
        wmid = split(wmid_ref[...])
        wout = split(wout_ref[...])

        def level(l, carry):
            xl = feat[step, l]
            z = bias_in + win[:, 0:1] * xl[0:1] + win[:, 1:2] * xl[1:2] + win[:, 2:3] * xl[2:3]
            h = jnp.tanh(z)
            hid1[step, l] = h
            g = jnp.tanh(dot3(wmid, split(h)) + bias_mid)
            hid2[step, l] = g
            stress[l] = GAIN * dot3(wout, split(g))
            return carry

        lax.fori_loop(0, 8, level, 0)

    def columns_of(ref, c):
        return jnp.stack([ref[:, c, e * lat : (e + 1) * lat] for e in range(columns)])

    def update(ext):
        sxx, sxy, syy = (columns_of(stress, c) for c in range(3))
        fx = dx(sxx) + dy(sxy[1:-1])
        fy = dx(sxy) + dy(syy[1:-1])
        u, v, t, s = (ext[:, f] for f in range(4))
        cu, cv = u[2:-2], v[2:-2]
        buoy = 0.6 * t - 0.4 * s
        nu = wet * (
            cu + DT * (cor * cv - PRESS * dx(buoy[1:-1]) + fx + VISC * lap(u[1:-1]))
        )
        nv = wet * (
            cv + DT * (-cor * nu - PRESS * dy(buoy[2:-2]) + fy + VISC * lap(v[1:-1]))
        )
        upd[:, 0] = nu
        upd[:, 1] = nv
        for f, q in ((2, t), (3, s)):
            upd[:, f] = wet * (
                q[2:-2]
                + DT * (-cu * dx(q[1:-1]) - cv * dy(q[2:-2]) + VISC * lap(q[1:-1]))
            )

    def back_closure(step, gu, gv, need_state):
        hu, hv = (DT * GAIN) * gu, (DT * GAIN) * gv
        ds = (dx_t(hu), dx_t(hv) - pad(dy(hu)), -pad(dy(hv)))
        for c in range(3):
            for e in range(columns):
                stress[:, c, e * lat : (e + 1) * lat] = ds[c][e]
        stress[:, 3:8, :] = jnp.zeros((8, 5, columns * lat), F32)
        wmidt = split(wmidt_ref[...])
        wint = split(wint_ref[...])

        def level(l, carry):
            d = stress[l]
            h, g = hid1[step, l], hid2[step, l]
            xl = split(feat[step, l])
            dg = woutt[:, 0:1] * d[0:1] + woutt[:, 1:2] * d[1:2] + woutt[:, 2:3] * d[2:3]
            dz2 = split(dg * (1.0 - g * g))
            dh = dot3(wmidt, dz2)
            dz1 = split(dh * (1.0 - h * h))
            gsend[0, 0:64] += dot3(dz2, split(h), True)
            gsend[0, 64:72] += dot3(xl, dz1, True)
            gsend[0, 72:80] += dot3(xl, dz2, True)
            gsend[0, 80:88] += dot3(split(d), split(g), True)
            if need_state:
                stress[l] = dot3(wint, dz1)
            return carry

        lax.fori_loop(0, 8, level, 0)

    gsend[0] = jnp.zeros(gsend.shape[1:], F32)

    finish(first_halo)
    ext = ext1[...]
    closure(0, ext)
    update(ext)
    for i in range(width):
        raw[2 + i] = upd[i]
    second_halo = halo(1, raw)
    b = [[upd[i, f] for f in range(4)] for i in range(width)]
    filter_start(0, b)
    mid = filter_finish(0, b)
    finish(second_halo)
    for f in range(4):
        for i in range(width):
            ext2[2 + i, f] = mid[i][f]
        for edge, near, out in (((2, 3), (1, 0), 0), ((9, 8), (10, 11), 1)):
            x0, x1 = mid[edge[0] - 2][f], mid[edge[1] - 2][f]
            b0 = b[edge[0] - 2][f]
            for place in near:
                got = raw[place, f]
                fresh = jnp.where(polar, (x0 - x1) + (x0 + (x0 - b0) * inv_k), got)
                ext2[place, f] = fresh
                x1, x0, b0 = x0, fresh, got

    closure(1, ext2[...])
    update(ext2[...])
    b = [[upd[i, f] for f in range(4)] for i in range(width)]
    filter_start(1, b)
    last = filter_finish(1, b)
    scaling = 1.0 / (8 * lat * width)
    b = []
    for i in range(width):
        weight = scaling * (1.0 + 2.0 * (me * width + i).astype(F32) / (n * width))
        cols = []
        for f in range(4):
            final_ref[f, :, i, :] = last[i][f]
            cols.append(weight * (last[i][f] - target_ref[f, :, i, :]))
        b.append(cols)
    filter_start(2, b)
    a = filter_finish(2, b)
    for i in range(width):
        for f in range(4):
            upd[i, f] = a[i][f]

    gv = wet * upd[:, 1]
    gu = wet * (upd[:, 0] - DT * cor * gv)
    back_closure(1, gu, gv, True)
    ext = ext2[...]
    u, v, t, s = (ext[:, f] for f in range(4))
    cu, cv = u[2:-2], v[2:-2]
    avort, ashear, astretch = (columns_of(stress, c) for c in range(3))
    au = pad(pad(gu) + (DT * VISC) * lap_t(gu) - dy(ashear - avort)) + dx_t(astretch)
    av = (
        pad(pad(gv + DT * cor * gu) + (DT * VISC) * lap_t(gv) + dy(astretch))
        + dx_t(avort + ashear)
    )
    buoy_adj = (-DT * PRESS) * (dx_t(gu) - pad(dy(gv)))
    for f, q, gain in ((2, t, 0.6), (3, s, -0.4)):
        gq = wet * upd[:, f]
        scaled = DT * gq
        au = au - pad(scaled * dx(q[1:-1]), 2)
        av = av - pad(scaled * dy(q[2:-2]), 2)
        aq = pad(gq + dy(cv * scaled)) + VISC * lap_t(scaled) - dx_t(cu * scaled)
        adj[:, f] = pad(aq + gain * buoy_adj)
    adj[:, 0] = au
    adj[:, 1] = av
    rims = exchange(
        2, adj.at[pl.ds(0, 2)], adj.at[pl.ds(10, 2)], rim.at[1], rim.at[0]
    )
    finish(rims)
    b = []
    for i in range(width):
        cols = []
        for f in range(4):
            value = adj[2 + i, f]
            if i < 2:
                value = value + rim[0, i, f]
            if i >= width - 2:
                value = value + rim[1, i - (width - 2), f]
            sens_ref[f, :, i, :] = value * float(8 * lat * width)
            cols.append(value)
        b.append(cols)
    filter_start(3, b)
    a = filter_finish(3, b)
    for i in range(width):
        for f in range(2):
            upd[i, f] = a[i][f]
    gv = wet * upd[:, 1]
    gu = wet * (upd[:, 0] - DT * cor * gv)
    back_closure(0, gu, gv, False)

    for r in range(steps):
        stride = 1 << r
        partner = me + stride * (1 - 2 * lax.rem(me // stride, 2))
        c = remote(gsend.at[r], grecv.at[r], red_send.at[r], red_recv.at[r], partner)
        c.start()
        c.wait()
        both = gsend[r] + grecv[r]
        if r + 1 < steps:
            gsend[r + 1] = both
        else:
            grad_ref[...] = both


def on_device(
    n, ocean_state, ocean_mask, polar_rows, target_state,
    weight_in, bias_in, weight_mid, bias_mid, weight_out,
):
    width, lat = ocean_state.shape[2], ocean_state.shape[3]
    hidden = weight_in.shape[0]
    table, hops = filter_tables(n, width, lat, polar_rows.shape[0])
    steps = n.bit_length() - 1
    wide = (width + 2) * lat
    vmem = pl.BlockSpec(memory_space=pltpu.VMEM)
    smem = pl.BlockSpec(memory_space=pltpu.SMEM)
    grid = lambda *lead: pltpu.VMEM(lead + (4, 8, lat), F32)
    dma = pltpu.SemaphoreType.DMA
    final, sens, grads = pl.pallas_call(
        functools.partial(kernel, n),
        out_shape=(
            jax.ShapeDtypeStruct(ocean_state.shape, F32),
            jax.ShapeDtypeStruct(ocean_state.shape, F32),
            jax.ShapeDtypeStruct((hidden + 24, hidden), F32),
        ),
        in_specs=[smem] + [vmem] * 13,
        out_specs=[vmem] * 3,
        scratch_shapes=[
            grid(width + 4),
            grid(width + 4),
            grid(width + 4),
            grid(width + 4),
            grid(2, 2),
            grid(width),
            pltpu.VMEM((2, 8, 8, wide), F32),
            pltpu.VMEM((8, 8, wide), F32),
            pltpu.VMEM((2, 8, hidden, wide), F32),
            pltpu.VMEM((2, 8, hidden, wide), F32),
            pltpu.VMEM((4, 8, lat), F32),
            pltpu.VMEM((4, n - 1, 8, lat), F32),
            pltpu.VMEM((steps, hidden + 24, hidden), F32),
            pltpu.VMEM((steps, hidden + 24, hidden), F32),
            dma((3, 2)),
            dma((3, 2)),
            dma((4,)),
            dma((4,)),
            dma((steps,)),
            dma((steps,)),
        ],
        compiler_params=pltpu.CompilerParams(
            collective_id=0, has_side_effects=True, vmem_limit_bytes=48 * 1024 * 1024
        ),
    )(
        polar_rows,
        ocean_state,
        ocean_mask.reshape(width, 1, lat),
        target_state,
        weight_in,
        jnp.pad(weight_in.T, ((0, 5), (0, 0))),
        bias_in.reshape(hidden, 1),
        weight_mid,
        weight_mid.T,
        bias_mid.reshape(hidden, 1),
        jnp.pad(weight_out, ((0, 5), (0, 0))),
        weight_out.T,
        table,
        hops,
    )
    return (
        final,
        sens,
        grads[hidden : hidden + 3].T,
        grads[hidden + 3],
        grads[:hidden],
        grads[hidden + 11],
        grads[hidden + 16 : hidden + 19],
    )


def solution(mesh):
    field = P(None, "grp", "lon", None)
    in_specs = (field, P("lon", None), P(), field, P(), P(), P(), P(), P())
    out_specs = (field, field, P("grp", None), P("grp"), P("grp", None), P("grp"), P("grp", None))
    return jax.shard_map(
        functools.partial(on_device, mesh.shape["lon"]),
        mesh=mesh, in_specs=in_specs, out_specs=out_specs, check_vma=False,
    )
```

```python
import functools

import jax
import jax.numpy as jnp
import numpy as np
from jax import lax
from jax.experimental import pallas as pl
from jax.experimental.pallas import tpu as pltpu
from jax.sharding import PartitionSpec as P

DT = 0.2
VISC = 0.05
PRESS = 0.3
GAIN = 0.3
F32 = jnp.float32
BF16 = jnp.bfloat16
MESH = pl.DeviceIdType.MESH


def filter_tables(n, width, lat, pole):
    total = n * width
    band = 2 * pole
    rows = np.arange(band, dtype=np.float64)
    k = (total / 8.0) ** 2 * (2.0 + 4.0 * rows / band)
    theta = 2.0 * np.arcsinh(0.5 / np.sqrt(k))
    power = lambda d: np.exp(-theta * d)
    norm = (1.0 - power(total)) * np.sqrt(1.0 + 4.0 * k)
    wide = lambda x: np.concatenate([np.zeros(lat - band), x])
    i = range(width)
    local = [wide((power(d) + power(total - d)) / norm) for d in i]
    east = [wide(power(width - 1 - d)) for d in i]
    west = [wide(power(d)) for d in i]
    from_west = [wide(power(d + 1) / norm) for d in i]
    from_east = [wide(power(width - d) / norm) for d in i]
    inverse = [wide(1.0 / k)]
    table = np.stack(local + east + west + from_west + from_east + inverse)
    table = np.broadcast_to(table[:, None, :], (len(table), 8, lat))
    hops = np.stack(
        [
            np.concatenate([power(width * (m - 1))] * 4 + [power(width * (n - m - 1))] * 4)
            for m in range(1, n)
        ]
    )
    hops = np.broadcast_to(hops[:, None, :], (n - 1, 8, lat))
    return table.astype(np.float32), hops.astype(np.float32)


def split(a):
    high = a.astype(BF16)
    return high, (a - high.astype(F32)).astype(BF16)


def left_side(a):
    high = a.astype(BF16).astype(F32)
    return jnp.concatenate([high, high, a - high], 1).astype(BF16)


def dot3(a, b):
    b = jnp.concatenate([b[0], b[1], b[0]], 0)
    return jnp.dot(a, b, preferred_element_type=F32)


def stacked(a):
    high = a.astype(BF16).astype(F32)
    return jnp.concatenate([a, a - high], 0).astype(BF16)


def outer(a, b):
    dims = (((1,), (1,)), ((), ()))
    return lax.dot_general(a, b, dims, preferred_element_type=F32)


def folded(acc, rows):
    turned = pltpu.roll(acc, 64, 1)
    return (acc[:rows] + (turned[:rows] + acc[rows:]))[:, :64]


def kernel(
    n,
    rows_ref,
    state_ref,
    mask_ref,
    target_ref,
    win_ref,
    wint_ref,
    bin_ref,
    wmid_ref,
    wmidt_ref,
    bmid_ref,
    wout_ref,
    woutt_ref,
    tab_ref,
    hop_ref,
    final_ref,
    sens_ref,
    grad_ref,
    ext1,
    raw,
    ext2,
    adj,
    rim,
    upd,
    feat,
    stress,
    hid1,
    hid2,
    sendv,
    recvv,
    gsend,
    grecv,
    acc_mid,
    acc_in,
    acc_out,
    halo_send,
    halo_recv,
    fil_send,
    fil_recv,
    red_send,
    red_recv,
):
    width = 8
    lat = 128
    me = lax.axis_index("lon")
    left, right = lax.rem(me + n - 1, n), lax.rem(me + 1, n)
    lane = lax.broadcasted_iota(jnp.int32, (1, 1, lat), 2)
    lane2 = lax.broadcasted_iota(jnp.int32, (8, lat), 1)
    steps = n.bit_length() - 1

    barrier = pltpu.get_barrier_semaphore()

    def greet(m, carry):
        pl.semaphore_signal(
            barrier, inc=1, device_id={"lon": lax.rem(me + m, n)}, device_id_type=MESH
        )
        return carry

    lax.fori_loop(1, n, greet, 0)

    for f in range(4):
        for i in range(width):
            ext1[2 + i, f] = state_ref[f, :, i, :]
    pl.semaphore_wait(barrier, n - 1)

    def remote(src, dst, ssem, rsem, dev):
        return pltpu.make_async_remote_copy(
            src_ref=src, dst_ref=dst, send_sem=ssem, recv_sem=rsem,
            device_id={"lon": dev}, device_id_type=MESH,
        )

    def exchange(which, src_l, src_r, dst_l, dst_r):
        a = remote(src_l, dst_l, halo_send.at[which, 0], halo_recv.at[which, 0], left)
        b = remote(src_r, dst_r, halo_send.at[which, 1], halo_recv.at[which, 1], right)
        a.start()
        b.start()
        return a, b

    def halo(which, ref):
        return exchange(
            which,
            ref.at[pl.ds(2, 2)],
            ref.at[pl.ds(8, 2)],
            ref.at[pl.ds(10, 2)],
            ref.at[pl.ds(0, 2)],
        )

    def finish(pair):
        for c in pair:
            c.wait()

    first_halo = halo(0, ext1)

    polar = lane2 == rows_ref[0]
    for j in range(1, rows_ref.shape[0]):
        polar = jnp.logical_or(polar, lane2 == rows_ref[j])
    wet = jnp.broadcast_to(mask_ref[...].astype(F32), (width, 8, lat))
    cor = 0.5 + 0.5 * (lane.astype(F32) + 0.5) / lat
    local = [
        jnp.where(polar, tab_ref[d], 1.0 if d == 0 else 0.0) for d in range(width)
    ]
    inv_k = tab_ref[5 * width]

    def dy_sides(x):
        up = jnp.where(lane == lat - 1, 0.0, pltpu.roll(x, lat - 1, 2))
        down = jnp.where(lane == 0, 0.0, pltpu.roll(x, 1, 2))
        return up, down

    def dy(x):
        up, down = dy_sides(x)
        return 0.5 * (up - down)

    def dx(x):
        return 0.5 * (x[2:] - x[:-2])

    def lap(x):
        up, down = dy_sides(x[1:-1])
        return x[2:] + x[:-2] + up + down - 4.0 * x[1:-1]

    def pad(x, count=1):
        zero = jnp.zeros((count,) + x.shape[1:], F32)
        return jnp.concatenate([zero, x, zero], 0)

    def dx_t(x):
        wide = pad(x, 2)
        return -0.5 * (wide[2:] - wide[:-2])

    def lap_t(x):
        return lap(pad(x, 2))

    def filter_start(which, b):
        packed = jnp.zeros((8, lat), F32)
        for q in range(8):
            f = q % 4
            base = width if q < 4 else 2 * width
            moment = b[0][f] * tab_ref[base]
            for i in range(1, width):
                moment += b[i][f] * tab_ref[base + i]
            shift = (16 * q + 16) % lat
            packed += pltpu.roll(moment, shift, 1) if shift else moment
        sendv[which] = packed

        def push(m, carry):
            remote(
                sendv.at[which], recvv.at[which, m - 1],
                fil_send.at[which], fil_recv.at[which], lax.rem(me + m, n),
            ).start()
            return carry

        lax.fori_loop(1, n, push, 0)

    def filter_finish(which, b):
        out = []
        for i in range(width):
            cols = []
            for f in range(4):
                acc = local[i] * b[0][f]
                for j in range(1, width):
                    acc += local[abs(i - j)] * b[j][f]
                cols.append(acc)
            out.append(cols)
        whole = remote(
            recvv.at[which], recvv.at[which], fil_send.at[which], fil_recv.at[which], right
        )
        whole.wait_recv()
        whole.wait_send()
        total = jnp.sum(recvv[which] * hop_ref[...], axis=0)
        for f in range(4):
            parts = []
            for q in (f, f + 4):
                shift = (lat - 16 - 16 * q) % lat
                parts.append(pltpu.roll(total, shift, 1) if shift else total)
            for i in range(width):
                out[i][f] = out[i][f] + jnp.where(
                    polar,
                    tab_ref[3 * width + i] * parts[0] + tab_ref[4 * width + i] * parts[1],
                    0.0,
                )
        return out

    columns = width + 2
    win = win_ref[...]
    woutt = woutt_ref[...]
    bias_in = bin_ref[...]
    bias_mid = bmid_ref[...]

    def closure(step, ext):
        u, v = ext[:, 0], ext[:, 1]
        du, dv = dx(u), dx(v)
        eu, ev = dy(u[1:-1]), dy(v[1:-1])
        x = (dv - eu, eu + dv, du - ev)
        for c in range(3):
            for e in range(columns):
                feat[step, :, c, e * lat : (e + 1) * lat] = x[c][e]
        feat[step, :, 3, :] = jnp.ones((8, columns * lat), F32)
        feat[step, :, 4:8, :] = jnp.zeros((8, 4, columns * lat), F32)
        wmid = left_side(wmid_ref[...])
        wout = left_side(wout_ref[...])

        def level(l, carry):
            xl = feat[step, l]
            z = bias_in + win[:, 0:1] * xl[0:1] + win[:, 1:2] * xl[1:2] + win[:, 2:3] * xl[2:3]
            h = jnp.tanh(z)
            hid1[step, l] = h
            g = jnp.tanh(dot3(wmid, split(h)) + bias_mid)
            hid2[step, l] = g
            stress[l] = GAIN * dot3(wout, split(g))
            return carry

        lax.fori_loop(0, 8, level, 0)

    def columns_of(ref, c):
        return jnp.stack([ref[:, c, e * lat : (e + 1) * lat] for e in range(columns)])

    def update(ext):
        sxx, sxy, syy = (columns_of(stress, c) for c in range(3))
        fx = dx(sxx) + dy(sxy[1:-1])
        fy = dx(sxy) + dy(syy[1:-1])
        u, v, t, s = (ext[:, f] for f in range(4))
        cu, cv = u[2:-2], v[2:-2]
        buoy = 0.6 * t - 0.4 * s
        nu = wet * (
            cu + DT * (cor * cv - PRESS * dx(buoy[1:-1]) + fx + VISC * lap(u[1:-1]))
        )
        nv = wet * (
            cv + DT * (-cor * nu - PRESS * dy(buoy[2:-2]) + fy + VISC * lap(v[1:-1]))
        )
        upd[:, 0] = nu
        upd[:, 1] = nv
        for f, q in ((2, t), (3, s)):
            upd[:, f] = wet * (
                q[2:-2]
                + DT * (-cu * dx(q[1:-1]) - cv * dy(q[2:-2]) + VISC * lap(q[1:-1]))
            )

    def back_closure(step, gu, gv, need_state):
        hu, hv = (DT * GAIN) * gu, (DT * GAIN) * gv
        ds = (dx_t(hu), dx_t(hv) - pad(dy(hu)), -pad(dy(hv)))
        for c in range(3):
            for e in range(columns):
                stress[:, c, e * lat : (e + 1) * lat] = ds[c][e]
        stress[:, 3:8, :] = jnp.zeros((8, 5, columns * lat), F32)
        wmidt = left_side(wmidt_ref[...])
        wint = left_side(wint_ref[...])

        def level(l, carry):
            d = stress[l]
            h, g = hid1[step, l], hid2[step, l]
            xl = stacked(feat[step, l])
            dg = woutt[:, 0:1] * d[0:1] + woutt[:, 1:2] * d[1:2] + woutt[:, 2:3] * d[2:3]
            dz2 = split(dg * (1.0 - g * g))
            dh = dot3(wmidt, dz2)
            dz1 = split(dh * (1.0 - h * h))
            two = jnp.concatenate(dz2, 0)
            acc_mid[...] += outer(two, stacked(h))
            acc_in[:, 0:128] += outer(xl, jnp.concatenate(dz1, 0))
            acc_in[:, 128:256] += outer(xl, two)
            acc_out[...] += outer(stacked(d), stacked(g))
            if need_state:
                stress[l] = dot3(wint, dz1)
            return carry

        lax.fori_loop(0, 8, level, 0)

    for acc in (acc_mid, acc_in, acc_out):
        acc[...] = jnp.zeros(acc.shape, F32)

    finish(first_halo)
    ext = ext1[...]
    closure(0, ext)
    update(ext)
    for i in range(width):
        raw[2 + i] = upd[i]
    second_halo = halo(1, raw)
    b = [[upd[i, f] for f in range(4)] for i in range(width)]
    filter_start(0, b)
    mid = filter_finish(0, b)
    finish(second_halo)
    for f in range(4):
        for i in range(width):
            ext2[2 + i, f] = mid[i][f]
        for edge, near, out in (((2, 3), (1, 0), 0), ((9, 8), (10, 11), 1)):
            x0, x1 = mid[edge[0] - 2][f], mid[edge[1] - 2][f]
            b0 = b[edge[0] - 2][f]
            for place in near:
                got = raw[place, f]
                fresh = jnp.where(polar, (x0 - x1) + (x0 + (x0 - b0) * inv_k), got)
                ext2[place, f] = fresh
                x1, x0, b0 = x0, fresh, got

    closure(1, ext2[...])
    update(ext2[...])
    b = [[upd[i, f] for f in range(4)] for i in range(width)]
    filter_start(1, b)
    last = filter_finish(1, b)
    scaling = 1.0 / (8 * lat * width)
    b = []
    for i in range(width):
        weight = scaling * (1.0 + 2.0 * (me * width + i).astype(F32) / (n * width))
        cols = []
        for f in range(4):
            final_ref[f, :, i, :] = last[i][f]
            cols.append(weight * (last[i][f] - target_ref[f, :, i, :]))
        b.append(cols)
    filter_start(2, b)
    a = filter_finish(2, b)
    for i in range(width):
        for f in range(4):
            upd[i, f] = a[i][f]

    gv = wet * upd[:, 1]
    gu = wet * (upd[:, 0] - DT * cor * gv)
    back_closure(1, gu, gv, True)
    ext = ext2[...]
    u, v, t, s = (ext[:, f] for f in range(4))
    cu, cv = u[2:-2], v[2:-2]
    avort, ashear, astretch = (columns_of(stress, c) for c in range(3))
    au = pad(pad(gu) + (DT * VISC) * lap_t(gu) - dy(ashear - avort)) + dx_t(astretch)
    av = (
        pad(pad(gv + DT * cor * gu) + (DT * VISC) * lap_t(gv) + dy(astretch))
        + dx_t(avort + ashear)
    )
    buoy_adj = (-DT * PRESS) * (dx_t(gu) - pad(dy(gv)))
    for f, q, gain in ((2, t, 0.6), (3, s, -0.4)):
        gq = wet * upd[:, f]
        scaled = DT * gq
        au = au - pad(scaled * dx(q[1:-1]), 2)
        av = av - pad(scaled * dy(q[2:-2]), 2)
        aq = pad(gq + dy(cv * scaled)) + VISC * lap_t(scaled) - dx_t(cu * scaled)
        adj[:, f] = pad(aq + gain * buoy_adj)
    adj[:, 0] = au
    adj[:, 1] = av
    rims = exchange(
        2, adj.at[pl.ds(0, 2)], adj.at[pl.ds(10, 2)], rim.at[1], rim.at[0]
    )
    finish(rims)
    b = []
    for i in range(width):
        cols = []
        for f in range(4):
            value = adj[2 + i, f]
            if i < 2:
                value = value + rim[0, i, f]
            if i >= width - 2:
                value = value + rim[1, i - (width - 2), f]
            sens_ref[f, :, i, :] = value * float(8 * lat * width)
            cols.append(value)
        b.append(cols)
    filter_start(3, b)
    a = filter_finish(3, b)
    for i in range(width):
        for f in range(2):
            upd[i, f] = a[i][f]
    gv = wet * upd[:, 1]
    gu = wet * (upd[:, 0] - DT * cor * gv)
    back_closure(0, gu, gv, False)

    gsend[0, 0:64] = folded(acc_mid[...], 64)
    gsend[0, 64:72] = folded(acc_in[:, 0:128], 8)
    gsend[0, 72:80] = folded(acc_in[:, 128:256], 8)
    gsend[0, 80:88] = folded(acc_out[...], 8)
    for r in range(steps):
        stride = 1 << r
        partner = me + stride * (1 - 2 * lax.rem(me // stride, 2))
        c = remote(gsend.at[r], grecv.at[r], red_send.at[r], red_recv.at[r], partner)
        c.start()
        c.wait()
        both = gsend[r] + grecv[r]
        if r + 1 < steps:
            gsend[r + 1] = both
        else:
            grad_ref[...] = both


def on_device(
    n, ocean_state, ocean_mask, polar_rows, target_state,
    weight_in, bias_in, weight_mid, bias_mid, weight_out,
):
    width, lat = ocean_state.shape[2], ocean_state.shape[3]
    hidden = weight_in.shape[0]
    table, hops = filter_tables(n, width, lat, polar_rows.shape[0])
    steps = n.bit_length() - 1
    wide = (width + 2) * lat
    vmem = pl.BlockSpec(memory_space=pltpu.VMEM)
    smem = pl.BlockSpec(memory_space=pltpu.SMEM)
    grid = lambda *lead: pltpu.VMEM(lead + (4, 8, lat), F32)
    dma = pltpu.SemaphoreType.DMA
    final, sens, grads = pl.pallas_call(
        functools.partial(kernel, n),
        out_shape=(
            jax.ShapeDtypeStruct(ocean_state.shape, F32),
            jax.ShapeDtypeStruct(ocean_state.shape, F32),
            jax.ShapeDtypeStruct((hidden + 24, hidden), F32),
        ),
        in_specs=[smem] + [vmem] * 13,
        out_specs=[vmem] * 3,
        scratch_shapes=[
            grid(width + 4),
            grid(width + 4),
            grid(width + 4),
            grid(width + 4),
            grid(2, 2),
            grid(width),
            pltpu.VMEM((2, 8, 8, wide), F32),
            pltpu.VMEM((8, 8, wide), F32),
            pltpu.VMEM((2, 8, hidden, wide), F32),
            pltpu.VMEM((2, 8, hidden, wide), F32),
            pltpu.VMEM((4, 8, lat), F32),
            pltpu.VMEM((4, n - 1, 8, lat), F32),
            pltpu.VMEM((steps, hidden + 24, hidden), F32),
            pltpu.VMEM((steps, hidden + 24, hidden), F32),
            pltpu.VMEM((2 * hidden, 2 * hidden), F32),
            pltpu.VMEM((16, 4 * hidden), F32),
            pltpu.VMEM((16, 2 * hidden), F32),
            dma((3, 2)),
            dma((3, 2)),
            dma((4,)),
            dma((4,)),
            dma((steps,)),
            dma((steps,)),
        ],
        compiler_params=pltpu.CompilerParams(
            collective_id=0, has_side_effects=True, vmem_limit_bytes=48 * 1024 * 1024
        ),
    )(
        polar_rows,
        ocean_state,
        ocean_mask.reshape(width, 1, lat),
        target_state,
        weight_in,
        jnp.pad(weight_in.T, ((0, 5), (0, 0))),
        bias_in.reshape(hidden, 1),
        weight_mid,
        weight_mid.T,
        bias_mid.reshape(hidden, 1),
        jnp.pad(weight_out, ((0, 5), (0, 0))),
        weight_out.T,
        table,
        hops,
    )
    return (
        final,
        sens,
        grads[hidden : hidden + 3].T,
        grads[hidden + 3],
        grads[:hidden],
        grads[hidden + 11],
        grads[hidden + 16 : hidden + 19],
    )


def solution(mesh):
    field = P(None, "grp", "lon", None)
    in_specs = (field, P("lon", None), P(), field, P(), P(), P(), P(), P())
    out_specs = (field, field, P("grp", None), P("grp"), P("grp", None), P("grp"), P("grp", None))
    return jax.shard_map(
        functools.partial(on_device, mesh.shape["lon"]),
        mesh=mesh, in_specs=in_specs, out_specs=out_specs, check_vma=False,
    )
```
